512 devices in a mesh: patch: 32 (over z, core), tensor: 8 (over y, x_lo), guidance: 2 (over x_hi).
Axes of the slice: x: 4 (x_hi: 2, x_lo: 2; x = x_hi * 2 + x_lo), y: 4, z: 16, core: 2. Of those that a mesh axis runs over, the one named last changes fastest.
Arguments:
- tokens: bfloat16 [4096, 3072], P('patch', 'tensor'), may hold values from -6 to 6
- modulation: float32 [3, 2, 3072], replicated, may hold values from -3 to 3
- w_qkv: bfloat16 [3, 3072, 2048], P(None, None, ('tensor', 'guidance')), may hold values from -0.109375 to 0.109375
- w_out: bfloat16 [2048, 3072], P(('tensor', 'guidance')), may hold values from -6 to 6
- stale: bfloat16 [2, 2, 4096, 2048], P(None, 'guidance', 'patch', 'tensor'), may hold values from -48 to 48
- text: bfloat16 [2, 2, 256, 2048], P(None, 'guidance', None, 'tensor'), may hold values from -6 to 6
Outputs:
- mixed: bfloat16 [4096, 3072], P('patch', 'tensor')
The draws below stay inside these ranges and needn't reach their ends.
All inputs are finite; a program needn't handle non-finite values.
Results may differ from the reference program's by a relative error of at most 0.02.
Values may be sent and summed in bfloat16 or wider, within the bound.
No kernel may reach another device: no remote copies, remote signals or barrier semaphores. Data moves between devices by JAX's collectives and lax.ppermute only.
A program may use at most 64 MiB of HBM per device.

```python
import jax
import jax.numpy as jnp
from jax import lax

D = 3072
HEADS = 16
HEAD = 128
TEXT = 256
TOK_DEV = 128
TOKENS = 4096
N_PATCH = 32


def draw_stale(key, part):
    key = jax.random.fold_in(key, 11)
    shape = (2, 2, TOKENS, HEADS * HEAD)
    values = jnp.clip(jax.random.normal(key, shape, jnp.float32), -6.0, 6.0)
    return values.astype(jnp.bfloat16)


def levels(rng, extent, cuts, low, top_value):
    def one(axis_at, shards_of):
        steps = jax.random.uniform(jax.random.fold_in(jax.random.fold_in(rng, 6), axis_at), (shards_of,), jnp.float32, low / len(cuts), top_value / len(cuts))
        return jnp.repeat(jnp.exp(steps), extent[axis_at] // shards_of).reshape((-1,) + (1,) * (len(extent) - axis_at - 1))

    loudness = one(*cuts[0])
    for cut in cuts[1:]:
        loudness = loudness * one(*cut)
    return loudness


def centred(own_key, extent, spread, reach, pieces=(), held_as=jnp.bfloat16):
    entries = jax.random.normal(own_key, extent, jnp.float32) * spread
    if len(pieces) > 0:
        entries = levels(own_key, extent, pieces, -0.22, 0.18) * entries
    return jnp.clip(entries, min=-reach, max=reach).astype(held_as)


def setup_inputs(seed: int = 0) -> dict:
    splits = jax.random.split(jax.random.key(seed), 7)
    tokens = centred(splits[0], (TOKENS, D), 1.0, 6.0, ((0, 32), (1, 8)))
    modulation = centred(splits[1], (3, 2, D), 0.5, 3.0, (), jnp.float32)
    w_qkv = centred(splits[2], (3, D, HEADS * HEAD), D ** -0.5, 0.109375, ((2, 16),))
    w_out = centred(splits[3], (HEADS * HEAD, D), 1.0, 6.0, ((0, 16),))
    stale = draw_stale(jax.random.fold_in(splits[6], 71), 0)
    text = centred(splits[5], (2, 2, TEXT, HEADS * HEAD), 1.0, 6.0, ((1, 2), (3, 8)))
    return {"tokens": tokens, "modulation": modulation, "w_qkv": w_qkv, "w_out": w_out, "stale": stale, "text": text}


GUIDE = 3.0
EPSILON = 1e-06

def head_normalize(projected):
    shaped = projected.reshape(projected.shape[0], HEADS, HEAD)
    scaled = shaped * lax.rsqrt(lax.optimization_barrier(jnp.mean(shaped * shaped, axis=-1, keepdims=True)) + EPSILON)
    return scaled.astype(jnp.bfloat16)

def one_pass(normed, modulation, w_qkv, w_out, stale, text, which):
    modulated = (normed * (1.0 + modulation[1, which]) + modulation[0, which]).astype(jnp.bfloat16)
    queries = head_normalize(jnp.dot(modulated, w_qkv[0], preferred_element_type=jnp.float32))
    fresh_keys = head_normalize(jnp.dot(modulated, w_qkv[1], preferred_element_type=jnp.float32))
    fresh_values = jnp.dot(modulated, w_qkv[2], preferred_element_type=jnp.float32).astype(jnp.bfloat16).reshape(TOKENS, HEADS, HEAD)
    stale_keys = stale[0, which].reshape(TOKENS, HEADS, HEAD)
    stale_values = stale[1, which].reshape(TOKENS, HEADS, HEAD)
    text_keys = text[0, which].reshape(TEXT, HEADS, HEAD)
    text_values = text[1, which].reshape(TEXT, HEADS, HEAD)

    def per_block(block_index):
        first_row = (block_index * TOK_DEV).astype(jnp.int32)
        block_queries = lax.dynamic_slice_in_dim(queries, first_row, TOK_DEV, 0)
        own_keys = lax.dynamic_slice_in_dim(fresh_keys, first_row, TOK_DEV, 0)
        own_values = lax.dynamic_slice_in_dim(fresh_values, first_row, TOK_DEV, 0)
        zero = jnp.zeros((), jnp.int32)
        all_keys = lax.dynamic_update_slice(stale_keys, own_keys, (first_row, zero, zero))
        all_values = lax.dynamic_update_slice(stale_values, own_values, (first_row, zero, zero))
        all_keys = jnp.concatenate([text_keys, all_keys], axis=0)
        all_values = jnp.concatenate([text_values, all_values], axis=0)
        scores = jnp.einsum('thd,khd->htk', block_queries.astype(jnp.float32), all_keys.astype(jnp.float32)) * HEAD ** (-0.5)
        top = lax.optimization_barrier(jnp.max(scores, axis=-1, keepdims=True))
        weights = jnp.exp(scores - top)
        totals = lax.optimization_barrier(jnp.sum(weights, axis=-1))
        summed = jnp.einsum('htk,khd->thd', weights.astype(jnp.bfloat16).astype(jnp.float32), all_values.astype(jnp.float32))
        return (summed / jnp.transpose(totals)[:, :, None]).astype(jnp.bfloat16)
    attended = lax.map(per_block, jnp.arange(N_PATCH, dtype=jnp.int32)).reshape(TOKENS, HEADS * HEAD)
    return jnp.dot(attended, w_out, preferred_element_type=jnp.float32)

def reference(tokens, modulation, w_qkv, w_out, stale, text):
    tokens_f32 = tokens.astype(jnp.float32)
    average = lax.optimization_barrier(jnp.mean(tokens_f32, axis=-1, keepdims=True))
    centered = tokens_f32 - average
    normed = centered * lax.rsqrt(lax.optimization_barrier(jnp.mean(centered * centered, axis=-1, keepdims=True)) + EPSILON)
    branch_cond = one_pass(normed, modulation, w_qkv, w_out, stale, text, 0)
    branch_uncond = one_pass(normed, modulation, w_qkv, w_out, stale, text, 1)
    mixed = tokens_f32 + GUIDE * modulation[2, 0] * branch_cond + (1.0 - GUIDE) * modulation[2, 1] * branch_uncond
    return mixed.astype(jnp.bfloat16)
```

```python
import math

import jax
import jax.numpy as jnp
from jax import lax
from jax.experimental import pallas as pl
from jax.experimental.pallas import tpu as pltpu
from jax.sharding import PartitionSpec as P

HEAD = 128
GUIDE = 3.0
EPSILON = 1e-06
NEGATIVE = -1e30
BASE = math.log2(math.e) / math.sqrt(HEAD)
BLOCK = 128
PARTS = 8
COLS = 384
SHARE = 4
FRESH = BLOCK // SHARE
ASK = BLOCK + 2 * FRESH
REPLY = 2 * BLOCK + 16
BF16 = jnp.bfloat16
F32 = jnp.float32
VMEM = 24 * 1024 * 1024


def nt(a, b):
    return lax.dot_general(a, b, (((1,), (1,)), ((), ())), preferred_element_type=F32)


def nn(a, b):
    return jnp.dot(a, b, preferred_element_type=F32)


def project_kernel(x_ref, mod_ref, w_ref, out_ref):
    total = jnp.zeros((BLOCK, 1), F32)
    for b in range(PARTS):
        total += jnp.sum(x_ref[b].astype(F32), axis=-1, keepdims=True)
    average = total * (1.0 / (PARTS * COLS))
    total = jnp.zeros((BLOCK, 1), F32)
    for b in range(PARTS):
        centered = x_ref[b].astype(F32) - average
        total += jnp.sum(centered * centered, axis=-1, keepdims=True)
    inverse = lax.rsqrt(total * (1.0 / (PARTS * COLS)) + EPSILON)
    sums = [jnp.zeros((2 * BLOCK, HEAD), F32) for _ in range(3)]
    for b in range(PARTS):
        cols = slice(b * COLS, (b + 1) * COLS)
        normed = (x_ref[b].astype(F32) - average) * inverse
        both = [
            (normed * (1.0 + mod_ref[1, p : p + 1, cols]) + mod_ref[0, p : p + 1, cols]).astype(BF16)
            for p in range(2)
        ]
        both = jnp.concatenate(both, axis=0)
        for i in range(3):
            sums[i] += nn(both, w_ref[i, cols, :])

    def head_norm(v):
        return (v * lax.rsqrt(jnp.mean(v * v, axis=-1, keepdims=True) + EPSILON)).astype(BF16)

    query, key, value = head_norm(sums[0]), head_norm(sums[1]), sums[2].astype(BF16)
    for p in range(2):
        for j in range(SHARE):
            d = p * SHARE + j
            rows = slice(p * BLOCK + j * FRESH, p * BLOCK + (j + 1) * FRESH)
            out_ref[d, 0:BLOCK, :] = query[p * BLOCK : (p + 1) * BLOCK]
            out_ref[d, BLOCK : BLOCK + FRESH, :] = key[rows]
            out_ref[d, BLOCK + FRESH : ASK, :] = value[rows]


def attend_kernel(ask_ref, kv0, kv1, kv2, kv3, text_ref, out_ref):
    own = lax.axis_index("za") * 2 + lax.axis_index("core")
    text_rows = text_ref.shape[1] // SHARE
    first = pl.multiple_of(own * text_rows, text_rows)
    query_rows = SHARE * BLOCK
    row_block = lax.broadcasted_iota(jnp.int32, (query_rows, 1), 0) // BLOCK
    col = lax.broadcasted_iota(jnp.int32, (1, 2 * BLOCK), 1)
    own_stale = (row_block == own) & (col < BLOCK)
    other_fresh = row_block != col[:, :BLOCK] // FRESH
    lane = lax.broadcasted_iota(jnp.int32, (1, HEAD), 1)
    stats = jnp.zeros((BLOCK, HEAD), F32)
    for h in range(2):
        cols = slice(h * HEAD, (h + 1) * HEAD)
        mine = slice(h * SHARE, (h + 1) * SHARE)
        query = ask_ref[mine, 0:BLOCK, :].reshape(query_rows, HEAD)
        scores, values = [], []
        for n, kv in enumerate((kv0, kv1, kv2, kv3)):
            s = nt(query, kv[:, 0, :, cols].reshape(2 * BLOCK, HEAD))
            if n == 0:
                s = jnp.where(own_stale, NEGATIVE, s)
            scores.append(s)
            values.append(kv[:, 1, :, cols].reshape(2 * BLOCK, HEAD))
        s = nt(query, ask_ref[mine, BLOCK : BLOCK + FRESH, :].reshape(BLOCK, HEAD))
        scores.append(jnp.where(other_fresh, NEGATIVE, s))
        values.append(ask_ref[mine, BLOCK + FRESH : ASK, :].reshape(BLOCK, HEAD))
        scores.append(nt(query, text_ref[0, pl.ds(first, text_rows), cols]))
        values.append(text_ref[1, pl.ds(first, text_rows), cols])
        top = jnp.max(scores[0], axis=-1, keepdims=True)
        for s in scores[1:]:
            top = jnp.maximum(top, jnp.max(s, axis=-1, keepdims=True))
        top = top * BASE
        total = jnp.zeros((query_rows, 1), F32)
        summed = jnp.zeros((query_rows, HEAD), F32)
        for s, v in zip(scores, values):
            weights = jnp.exp2(s * BASE - top)
            total += jnp.sum(weights, axis=-1, keepdims=True)
            summed += nn(weights.astype(BF16), v)
        summed = (summed / total).astype(BF16)
        level = top + jnp.log2(total)
        high = level.astype(BF16).astype(F32)
        middle = (level - high).astype(BF16).astype(F32)
        low = level - high - middle
        for b in range(SHARE):
            rows = slice(b * BLOCK, (b + 1) * BLOCK)
            for g in range(2):
                out_ref[g * SHARE + b, h * BLOCK : (h + 1) * BLOCK, :] = summed[rows]
            for i, piece in enumerate((high, middle, low)):
                stats = jnp.where(lane == 16 * b + 3 * h + i, piece[rows], stats)
    stats = jnp.transpose(stats).astype(BF16)
    for b in range(SHARE):
        for g in range(2):
            out_ref[g * SHARE + b, 2 * BLOCK : REPLY, :] = stats[16 * b : 16 * b + 16]


def output_kernel(reply_ref, mod_ref, w_ref, out_ref):
    stats = jnp.concatenate([reply_ref[s, 2 * BLOCK : REPLY, :].astype(F32) for s in range(2 * SHARE)], axis=0)
    stats = jnp.transpose(stats)
    attended = []
    for p in range(2):
        heads = []
        for h in range(2):
            levels = []
            for j in range(SHARE):
                c = 16 * (p * SHARE + j) + 3 * h
                levels.append(stats[:, c : c + 1] + stats[:, c + 1 : c + 2] + stats[:, c + 2 : c + 3])
            top = jnp.maximum(jnp.maximum(levels[0], levels[1]), jnp.maximum(levels[2], levels[3]))
            shares = [jnp.exp2(level - top) for level in levels]
            total = shares[0] + shares[1] + shares[2] + shares[3]
            summed = jnp.zeros((BLOCK, HEAD), F32)
            for j in range(SHARE):
                part = reply_ref[p * SHARE + j, h * BLOCK : (h + 1) * BLOCK, :].astype(F32)
                summed += shares[j] * part
            heads.append((summed / total).astype(BF16))
        attended.append(jnp.concatenate(heads, axis=1))
    attended = jnp.concatenate(attended, axis=0)
    for b in range(PARTS):
        cols = slice(b * COLS, (b + 1) * COLS)
        branch = nn(attended, w_ref[:, cols])
        mixed = (GUIDE * mod_ref[2, 0:1, cols]) * branch[:BLOCK]
        mixed += ((1.0 - GUIDE) * mod_ref[2, 1:2, cols]) * branch[BLOCK:]
        out_ref[b] = mixed.astype(BF16)


def finish_kernel(parts_ref, tokens_ref, out_ref):
    total = tokens_ref[...].astype(F32)
    for b in range(PARTS):
        total += parts_ref[b].astype(F32)
    out_ref[...] = total.astype(BF16)


def call(kernel, shape, *operands):
    return pl.pallas_call(
        kernel,
        out_shape=jax.ShapeDtypeStruct(shape, BF16),
        compiler_params=pltpu.CompilerParams(vmem_limit_bytes=VMEM),
    )(*operands)


def shift(x, axes, count, step):
    return lax.ppermute(x, axes, [(i, (i + step) % count) for i in range(count)])


def local(tokens, modulation, w_qkv, w_out, stale, text):
    w_heads = lax.all_gather(w_out, "guidance", axis=0, tiled=True)
    own = stale.reshape(2, BLOCK, 2 * HEAD)
    far = shift(own, "zf", 4, 2)
    features = lax.all_to_all(
        jnp.broadcast_to(tokens[None], (PARTS, BLOCK, COLS)), "tensor", 0, 0
    )
    pair = jnp.stack([own, far])
    pair, features = lax.optimization_barrier((pair, features))
    quad = shift(pair, "zf", 4, 1)
    up = shift(pair, ("zf", "zb"), 8, 1)
    down = shift(pair, ("zf", "zb"), 8, -1)
    ask = call(project_kernel, (2 * SHARE, ASK, HEAD), features, modulation, w_qkv)
    group = ("guidance", "za", "core")
    ask = lax.all_to_all(ask, group, 0, 0)
    text = text.reshape(2, -1, 2 * HEAD)
    reply = call(attend_kernel, (2 * SHARE, REPLY, HEAD), ask, pair, quad, up, down, text)
    reply = lax.all_to_all(reply, group, 0, 0)
    parts = call(output_kernel, (PARTS, BLOCK, COLS), reply, modulation, w_heads)
    parts = lax.all_to_all(parts, "tensor", 0, 0)
    return call(finish_kernel, (BLOCK, COLS), parts, tokens)


def solution(mesh):
    fine = jax.sharding.Mesh(
        mesh.devices.reshape(4, 2, 2, 2, 8, 2), ("zf", "zb", "za", "core", "tensor", "guidance")
    )
    patch = ("zf", "zb", "za", "core")
    in_specs = (
        P(patch, "tensor"),
        P(),
        P(None, None, ("tensor", "guidance")),
        P(("tensor", "guidance"), None),
        P(None, "guidance", patch, "tensor"),
        P(None, "guidance", None, "tensor"),
    )
    return jax.shard_map(
        local, mesh=fine, in_specs=in_specs, out_specs=P(patch, "tensor"), check_vma=False
    )
```

```python
import math

import jax
import jax.numpy as jnp
from jax import lax
from jax.experimental import pallas as pl
from jax.experimental.pallas import tpu as pltpu
from jax.sharding import PartitionSpec as P

HEAD = 128
GUIDE = 3.0
EPSILON = 1e-06
NEGATIVE = -1e30
BASE = math.log2(math.e) / math.sqrt(HEAD)
BLOCK = 128
PARTS = 8
COLS = 384
SHARE = 2
FRESH = BLOCK // SHARE
ASK = BLOCK + 2 * FRESH
REPLY = 2 * BLOCK + 16
BF16 = jnp.bfloat16
F32 = jnp.float32
VMEM = 24 * 1024 * 1024


def nt(a, b):
    return lax.dot_general(a, b, (((1,), (1,)), ((), ())), preferred_element_type=F32)


def nn(a, b):
    return jnp.dot(a, b, preferred_element_type=F32)


def project_kernel(x_ref, mod_ref, w_ref, out_ref):
    total = jnp.zeros((BLOCK, 1), F32)
    for b in range(PARTS):
        total += jnp.sum(x_ref[b].astype(F32), axis=-1, keepdims=True)
    average = total * (1.0 / (PARTS * COLS))
    total = jnp.zeros((BLOCK, 1), F32)
    for b in range(PARTS):
        centered = x_ref[b].astype(F32) - average
        total += jnp.sum(centered * centered, axis=-1, keepdims=True)
    inverse = lax.rsqrt(total * (1.0 / (PARTS * COLS)) + EPSILON)
    sums = [jnp.zeros((2 * BLOCK, HEAD), F32) for _ in range(3)]
    for b in range(PARTS):
        cols = slice(b * COLS, (b + 1) * COLS)
        normed = (x_ref[b].astype(F32) - average) * inverse
        both = [
            (normed * (1.0 + mod_ref[1, p : p + 1, cols]) + mod_ref[0, p : p + 1, cols]).astype(BF16)
            for p in range(2)
        ]
        both = jnp.concatenate(both, axis=0)
        for i in range(3):
            sums[i] += nn(both, w_ref[i, cols, :])

    def head_norm(v):
        return (v * lax.rsqrt(jnp.mean(v * v, axis=-1, keepdims=True) + EPSILON)).astype(BF16)

    query, key, value = head_norm(sums[0]), head_norm(sums[1]), sums[2].astype(BF16)
    for p in range(2):
        for j in range(SHARE):
            d = p * SHARE + j
            rows = slice(p * BLOCK + j * FRESH, p * BLOCK + (j + 1) * FRESH)
            out_ref[d, 0:BLOCK, :] = query[p * BLOCK : (p + 1) * BLOCK]
            out_ref[d, BLOCK : BLOCK + FRESH, :] = key[rows]
            out_ref[d, BLOCK + FRESH : ASK, :] = value[rows]


def attend_kernel(ask_ref, kv_ref, text_ref, out_ref):
    own = lax.axis_index("za")
    block = lax.axis_index("zf") * 4 + lax.axis_index("zb") * 2 + lax.axis_index("core")
    text_rows = text_ref.shape[1] // SHARE
    first = pl.multiple_of(own * text_rows, text_rows)
    query_rows = SHARE * BLOCK
    row_block = lax.broadcasted_iota(jnp.int32, (query_rows, 1), 0) // BLOCK
    col = lax.broadcasted_iota(jnp.int32, (1, 2 * BLOCK), 1)
    own_block = jnp.where(row_block == own, block, -1)
    other_fresh = row_block != col[:, :BLOCK] // FRESH
    lane = lax.broadcasted_iota(jnp.int32, (1, HEAD), 1)
    stats = jnp.zeros((BLOCK, HEAD), F32)
    for h in range(2):
        cols = slice(h * HEAD, (h + 1) * HEAD)
        mine = slice(h * SHARE, (h + 1) * SHARE)
        query = ask_ref[mine, 0:BLOCK, :].reshape(query_rows, HEAD)
        scores, values = [], []
        for n in range(0, kv_ref.shape[0], 2):
            s = nt(query, kv_ref[n : n + 2, 0, :, cols].reshape(2 * BLOCK, HEAD))
            scores.append(jnp.where(own_block == col // BLOCK + n, NEGATIVE, s))
            values.append(kv_ref[n : n + 2, 1, :, cols].reshape(2 * BLOCK, HEAD))
        s = nt(query, ask_ref[mine, BLOCK : BLOCK + FRESH, :].reshape(BLOCK, HEAD))
        scores.append(jnp.where(other_fresh, NEGATIVE, s))
        values.append(ask_ref[mine, BLOCK + FRESH : ASK, :].reshape(BLOCK, HEAD))
        scores.append(nt(query, text_ref[0, pl.ds(first, text_rows), cols]))
        values.append(text_ref[1, pl.ds(first, text_rows), cols])
        top = jnp.max(scores[0], axis=-1, keepdims=True)
        for s in scores[1:]:
            top = jnp.maximum(top, jnp.max(s, axis=-1, keepdims=True))
        top = top * BASE
        total = jnp.zeros((query_rows, 1), F32)
        summed = jnp.zeros((query_rows, HEAD), F32)
        for s, v in zip(scores, values):
            weights = jnp.exp2(s * BASE - top)
            total += jnp.sum(weights, axis=-1, keepdims=True)
            summed += nn(weights.astype(BF16), v)
        summed = (summed / total).astype(BF16)
        level = top + jnp.log2(total)
        high = level.astype(BF16).astype(F32)
        middle = (level - high).astype(BF16).astype(F32)
        low = level - high - middle
        for b in range(SHARE):
            rows = slice(b * BLOCK, (b + 1) * BLOCK)
            for g in range(2):
                out_ref[g * SHARE + b, h * BLOCK : (h + 1) * BLOCK, :] = summed[rows]
            for i, piece in enumerate((high, middle, low)):
                stats = jnp.where(lane == 16 * b + 3 * h + i, piece[rows], stats)
    stats = jnp.transpose(stats).astype(BF16)
    for b in range(SHARE):
        for g in range(2):
            out_ref[g * SHARE + b, 2 * BLOCK : REPLY, :] = stats[16 * b : 16 * b + 16]


def output_kernel(reply_ref, mod_ref, w_ref, other_ref, out_ref):
    flip = lax.axis_index("guidance") == 1
    stats = [reply_ref[s, 2 * BLOCK : REPLY, :].astype(F32) for s in range(2 * SHARE)]
    stats.append(jnp.zeros((HEAD - 32 * SHARE, HEAD), F32))
    stats = jnp.transpose(jnp.concatenate(stats, axis=0))
    attended = []
    for p in range(2):
        heads = []
        for h in range(2):
            levels = []
            for j in range(SHARE):
                c = 16 * (p * SHARE + j) + 3 * h
                levels.append(stats[:, c : c + 1] + stats[:, c + 1 : c + 2] + stats[:, c + 2 : c + 3])
            top = jnp.maximum(levels[0], levels[1])
            shares = [jnp.exp2(level - top) for level in levels]
            total = shares[0] + shares[1]
            summed = jnp.zeros((BLOCK, HEAD), F32)
            for j in range(SHARE):
                part = reply_ref[p * SHARE + j, h * BLOCK : (h + 1) * BLOCK, :].astype(F32)
                summed += shares[j] * part
            heads.append(summed / total)
        attended.append(heads)
    own = [jnp.where(flip, heads[1], heads[0]).astype(BF16) for heads in attended]
    other = [jnp.where(flip, heads[0], heads[1]).astype(BF16) for heads in attended]
    attended = jnp.concatenate([jnp.concatenate(own, axis=0), jnp.concatenate(other, axis=0)], axis=1)
    for b in range(PARTS):
        cols = slice(b * COLS, (b + 1) * COLS)
        weights = jnp.concatenate([w_ref[:, cols], other_ref[:, cols]], axis=0)
        branch = nn(attended, weights)
        mixed = (GUIDE * mod_ref[2, 0:1, cols]) * branch[:BLOCK]
        mixed += ((1.0 - GUIDE) * mod_ref[2, 1:2, cols]) * branch[BLOCK:]
        out_ref[b] = mixed.astype(BF16)


def finish_kernel(parts_ref, tokens_ref, out_ref):
    total = tokens_ref[...].astype(F32)
    for b in range(PARTS):
        total += parts_ref[b].astype(F32)
    out_ref[...] = total.astype(BF16)


def call(kernel, shape, *operands):
    return pl.pallas_call(
        kernel,
        out_shape=jax.ShapeDtypeStruct(shape, BF16),
        compiler_params=pltpu.CompilerParams(vmem_limit_bytes=VMEM),
    )(*operands)


def together(run, *operands):
    shapes = jax.eval_shape(run, *operands)
    return lax.cond(
        lax.axis_index("za") < 2,
        run,
        lambda *_: jax.tree.map(lambda s: jnp.zeros(s.shape, s.dtype), shapes),
        *operands,
    )


def local(tokens, modulation, w_qkv, w_out, stale, text):
    group = ("guidance", "za")
    stale = lax.all_gather(stale.reshape(2, BLOCK, 2 * HEAD), ("zf", "zb", "core"))

    def ask(tokens, modulation, w_qkv, w_out):
        features = lax.all_to_all(
            jnp.broadcast_to(tokens[None], (PARTS, BLOCK, COLS)), "tensor", 0, 0
        )
        message = call(project_kernel, (2 * SHARE, ASK, HEAD), features, modulation, w_qkv)
        message = lax.all_to_all(message, group, 0, 0)
        message, w_out = lax.optimization_barrier((message, w_out))
        return message, lax.ppermute(w_out, "guidance", [(0, 1), (1, 0)])

    message, other_w = together(ask, tokens, modulation, w_qkv, w_out)
    text = text.reshape(2, -1, 2 * HEAD)
    message = call(attend_kernel, (2 * SHARE, REPLY, HEAD), message, stale, text)
    message = lax.all_to_all(message, group, 0, 0)
    parts = call(output_kernel, (PARTS, BLOCK, COLS), message, modulation, w_out, other_w)
    parts = lax.all_to_all(parts, "tensor", 0, 0)
    return call(finish_kernel, (BLOCK, COLS), parts, tokens)


def solution(mesh):
    fine = jax.sharding.Mesh(
        mesh.devices.reshape(4, 2, 2, 2, 8, 2), ("zf", "zb", "za", "core", "tensor", "guidance")
    )
    patch = ("zf", "zb", "za", "core")
    in_specs = (
        P(patch, "tensor"),
        P(),
        P(None, None, ("tensor", "guidance")),
        P(("tensor", "guidance"), None),
        P(None, "guidance", patch, "tensor"),
        P(None, "guidance", None, "tensor"),
    )
    return jax.shard_map(
        local, mesh=fine, in_specs=in_specs, out_specs=P(patch, "tensor"), check_vma=False
    )
```

```python
import math

import jax
import jax.numpy as jnp
from jax import lax
from jax.experimental import pallas as pl
from jax.experimental.pallas import tpu as pltpu
from jax.sharding import PartitionSpec as P

HEAD = 128
GUIDE = 3.0
EPSILON = 1e-06
NEGATIVE = -1e30
BASE = math.log2(math.e) / math.sqrt(HEAD)
BLOCK = 128
PARTS = 8
COLS = 384
SHARE = 4
CHIPS = 2
QUERIES = SHARE * BLOCK
LEAF = BLOCK + 16
REPLY = 2 * BLOCK + 16
BF16 = jnp.bfloat16
F32 = jnp.float32
VMEM = 24 * 1024 * 1024


def nt(a, b):
    return lax.dot_general(a, b, (((1,), (1,)), ((), ())), preferred_element_type=F32)


def nn(a, b):
    return jnp.dot(a, b, preferred_element_type=F32)


def project_kernel(x_ref, mod_ref, w_ref, own_ref, away_ref):
    total = jnp.zeros((BLOCK, 1), F32)
    for b in range(PARTS):
        total += jnp.sum(x_ref[b].astype(F32), axis=-1, keepdims=True)
    average = total * (1.0 / (PARTS * COLS))
    total = jnp.zeros((BLOCK, 1), F32)
    for b in range(PARTS):
        centered = x_ref[b].astype(F32) - average
        total += jnp.sum(centered * centered, axis=-1, keepdims=True)
    inverse = lax.rsqrt(total * (1.0 / (PARTS * COLS)) + EPSILON)
    sums = [jnp.zeros((2 * BLOCK, HEAD), F32) for _ in range(3)]
    for b in range(PARTS):
        cols = slice(b * COLS, (b + 1) * COLS)
        normed = (x_ref[b].astype(F32) - average) * inverse
        both = [
            (normed * (1.0 + mod_ref[1, p : p + 1, cols]) + mod_ref[0, p : p + 1, cols]).astype(BF16)
            for p in range(2)
        ]
        both = jnp.concatenate(both, axis=0)
        for i in range(3):
            sums[i] += nn(both, w_ref[i, cols, :])

    def head_norm(v, scale):
        inverse = lax.rsqrt(jnp.mean(v * v, axis=-1, keepdims=True) + EPSILON) * scale
        return (v * inverse).astype(BF16)

    heads = head_norm(sums[0], BASE), head_norm(sums[1], 1.0), sums[2].astype(BF16)
    guidance = lax.axis_index("guidance")
    for p in range(2):
        rows = slice(p * BLOCK, (p + 1) * BLOCK)

        @pl.when(guidance == p)
        def _():
            for i in range(3):
                own_ref[i] = heads[i][rows]

        @pl.when(guidance != p)
        def _():
            for i in range(3):
                away_ref[i] = heads[i][rows]


def split_level(level):
    high = level.astype(BF16).astype(F32)
    middle = (level - high).astype(BF16).astype(F32)
    return high, middle, level - high - middle


def read_levels(stats):
    count = sum(s.shape[0] for s in stats) // 16
    stats = [s.astype(F32) for s in stats] + [jnp.zeros((HEAD - 16 * count, HEAD), F32)]
    stats = jnp.transpose(jnp.concatenate(stats, axis=0))
    return [
        [sum(stats[:, 16 * j + 3 * h + i : 16 * j + 3 * h + i + 1] for i in range(3)) for h in range(2)]
        for j in range(count)
    ]


def join(levels, parts):
    top = jnp.maximum(levels[0], levels[1])
    shares = [jnp.exp2(level - top) for level in levels]
    total = shares[0] + shares[1]
    joined = shares[0] * parts[0].astype(F32) + shares[1] * parts[1].astype(F32)
    return joined / total, top + jnp.log2(total)


def attend_kernel(query_ref, fresh_ref, kv0, kv1, kv2, kv3, kv4, text_ref, out_ref):
    own = lax.axis_index("za") * 2 + lax.axis_index("core")
    text_rows = text_ref.shape[1] // SHARE
    first = pl.multiple_of(own * text_rows, text_rows)
    row_block = lax.broadcasted_iota(jnp.int32, (QUERIES, 1), 0) // BLOCK
    col = lax.broadcasted_iota(jnp.int32, (1, 2 * BLOCK), 1)
    own_stale = (row_block == own) & (col < BLOCK)
    other_rows = row_block != own
    lane = lax.broadcasted_iota(jnp.int32, (1, HEAD), 1)
    stats = jnp.zeros((BLOCK, HEAD), F32)
    for h in range(2):
        cols = slice(h * HEAD, (h + 1) * HEAD)
        query = query_ref[:, h].reshape(QUERIES, HEAD)
        scores, values = [], []
        for n, kv in enumerate((kv0, kv1, kv2)):
            s = nt(query, kv[:, 0, :, cols].reshape(2 * BLOCK, HEAD))
            if n == 0:
                s = jnp.where(own_stale, NEGATIVE, s)
            scores.append(s)
            values.append(kv[:, 1, :, cols].reshape(2 * BLOCK, HEAD))
        for kv in (kv3, kv4):
            scores.append(nt(query, kv[0, :, cols]))
            values.append(kv[1, :, cols])
        scores.append(jnp.where(other_rows, NEGATIVE, nt(query, fresh_ref[h, 1])))
        values.append(fresh_ref[h, 2])
        scores.append(nt(query, text_ref[0, pl.ds(first, text_rows), cols]))
        values.append(text_ref[1, pl.ds(first, text_rows), cols])
        top = jnp.max(scores[0], axis=-1, keepdims=True)
        for s in scores[1:]:
            top = jnp.maximum(top, jnp.max(s, axis=-1, keepdims=True))
        total = jnp.zeros((QUERIES, 1), F32)
        summed = jnp.zeros((QUERIES, HEAD), F32)
        for s, v in zip(scores, values):
            weights = jnp.exp2(s - top)
            total += jnp.sum(weights, axis=-1, keepdims=True)
            summed += nn(weights.astype(BF16), v)
        summed = (summed / total).astype(BF16)
        pieces = split_level(top + jnp.log2(total))
        for b in range(SHARE):
            rows = slice(b * BLOCK, (b + 1) * BLOCK)
            out_ref[b, h * BLOCK : (h + 1) * BLOCK, :] = summed[rows]
            for i, piece in enumerate(pieces):
                stats = jnp.where(lane == 16 * b + 3 * h + i, piece[rows], stats)
    stats = jnp.transpose(stats).astype(BF16)
    for b in range(SHARE):
        out_ref[b, 2 * BLOCK : REPLY, :] = stats[16 * b : 16 * b + 16]


def join_kernel(mine_ref, cores_ref, out_ref):
    core = lax.axis_index("core")
    lane = lax.broadcasted_iota(jnp.int32, (1, HEAD), 1)
    stats = jnp.zeros((BLOCK, HEAD), F32)
    mine = [mine_ref[pl.ds(2 * b + core, 1)][0] for b in range(CHIPS)]
    other = [cores_ref[pl.ds(1 - core, 1), b][0] for b in range(CHIPS)]
    levels = read_levels([m[2 * BLOCK : REPLY] for m in mine + other])
    for b in range(CHIPS):
        for h in range(2):
            rows = slice(h * BLOCK, (h + 1) * BLOCK)
            joined, level = join(
                [levels[b][h], levels[CHIPS + b][h]], [mine[b][rows], other[b][rows]]
            )
            out_ref[h * CHIPS + b, 0:BLOCK, :] = joined.astype(BF16)
            for i, piece in enumerate(split_level(level)):
                stats = jnp.where(lane == 16 * (h * CHIPS + b) + i, piece, stats)
    stats = jnp.transpose(stats).astype(BF16)
    for d in range(2 * CHIPS):
        out_ref[d, BLOCK:LEAF, :] = stats[16 * d : 16 * d + 16]


def output_kernel(reply_ref, mod_ref, w_ref, out_ref):
    levels = read_levels([reply_ref[s, BLOCK:LEAF, :] for s in range(2 * CHIPS)])
    attended = []
    for p in range(2):
        pair = (p * CHIPS, p * CHIPS + 1)
        joined, _ = join([levels[s][0] for s in pair], [reply_ref[s, 0:BLOCK, :] for s in pair])
        attended.append(joined.astype(BF16))
    attended = jnp.concatenate(attended, axis=0)
    for b in range(PARTS):
        cols = slice(b * COLS, (b + 1) * COLS)
        branch = nn(attended, w_ref[:, cols])
        mixed = (GUIDE * mod_ref[2, 0:1, cols]) * branch[:BLOCK]
        mixed += ((1.0 - GUIDE) * mod_ref[2, 1:2, cols]) * branch[BLOCK:]
        out_ref[b] = mixed.astype(BF16)


def sum_kernel(parts_ref, out_ref):
    total = jnp.zeros(out_ref.shape, F32)
    for b in range(PARTS):
        total += parts_ref[b].astype(F32)
    out_ref[...] = total.astype(BF16)


def finish_kernel(heads_ref, tokens_ref, out_ref):
    total = tokens_ref[...].astype(F32) + heads_ref[0].astype(F32) + heads_ref[1].astype(F32)
    out_ref[...] = total.astype(BF16)


def call(kernel, shape, *operands):
    out_shape = shape
    if isinstance(shape, tuple):
        out_shape = jax.ShapeDtypeStruct(shape, BF16)
    return pl.pallas_call(
        kernel,
        out_shape=out_shape,
        compiler_params=pltpu.CompilerParams(vmem_limit_bytes=VMEM),
    )(*operands)


def shift(x, axes, count, step):
    return lax.ppermute(x, axes, [(i, (i + step) % count) for i in range(count)])


def by_core(i):
    zf, core = divmod(i, 2)
    return (zf + 1 - 2 * core) % 4 * 2 + core


def together(run, *operands):
    shapes = jax.eval_shape(run, *operands)
    return lax.cond(
        lax.axis_index("za") < 2,
        run,
        lambda *_: jax.tree.map(lambda s: jnp.zeros(s.shape, s.dtype), shapes),
        *operands,
    )


def local(tokens, modulation, w_qkv, w_out, stale, text):
    core = lax.axis_index("core")
    own = stale.reshape(2, BLOCK, 2 * HEAD)
    text = text.reshape(2, -1, 2 * HEAD)
    behind = shift(own, "zf", 4, 1)
    ahead = shift(own, "zf", 4, -1)

    def project(tokens, modulation, w_qkv):
        features = lax.all_to_all(
            jnp.broadcast_to(tokens[None], (PARTS, BLOCK, COLS)), "tensor", 0, 0
        )
        w_qkv = pltpu.with_memory_space_constraint(w_qkv, pltpu.VMEM)
        one_pass = jax.ShapeDtypeStruct((3, BLOCK, HEAD), BF16)
        return call(project_kernel, [one_pass, one_pass], features, modulation, w_qkv)

    own_pass, away = together(project, tokens, modulation, w_qkv)
    away, behind, ahead = lax.optimization_barrier((away, behind, ahead))
    up = jnp.stack([own, behind])
    down = jnp.stack([own, ahead])
    far = lax.ppermute(
        jnp.where(core == 0, behind, ahead), ("zf", "core"), [(i, by_core(i)) for i in range(8)]
    )
    below = shift(up, ("zf", "zb"), 8, 1)
    above = shift(down, ("zf", "zb"), 8, -1)

    def hand_out(own_pass, away):
        heads = lax.all_gather(away, "guidance")
        mine = lax.axis_index("guidance")
        first = jnp.where(mine == 0, own_pass, heads[0])
        second = jnp.where(mine == 0, heads[1], own_pass)
        fresh = jnp.stack([first, second])
        return lax.all_gather(fresh[:, 0], ("za", "core")), fresh

    queries, fresh = together(hand_out, own_pass, away)
    mine = call(
        attend_kernel, (SHARE, REPLY, HEAD), queries, fresh, up, below, above, ahead, far, text
    )
    away = jnp.where(core == 0, mine[1::2], mine[0::2])
    message = call(join_kernel, (2 * CHIPS, LEAF, HEAD), mine, lax.all_gather(away, "core"))
    message = lax.all_to_all(message, ("guidance", "za"), 0, 0)
    parts = call(output_kernel, (PARTS, BLOCK, COLS), message, modulation, w_out)
    parts = lax.all_to_all(parts, "tensor", 0, 0)
    heads = lax.all_gather(call(sum_kernel, (BLOCK, COLS), parts), "guidance")
    return call(finish_kernel, (BLOCK, COLS), heads, tokens)


def solution(mesh):
    fine = jax.sharding.Mesh(
        mesh.devices.reshape(4, 2, 2, 2, 8, 2), ("zf", "zb", "za", "core", "tensor", "guidance")
    )
    patch = ("zf", "zb", "za", "core")
    in_specs = (
        P(patch, "tensor"),
        P(),
        P(None, None, ("tensor", "guidance")),
        P(("tensor", "guidance"), None),
        P(None, "guidance", patch, "tensor"),
        P(None, "guidance", None, "tensor"),
    )
    return jax.shard_map(
        local, mesh=fine, in_specs=in_specs, out_specs=P(patch, "tensor"), check_vma=False
    )
```

```python
import math

import jax
import jax.numpy as jnp
from jax import lax
from jax.experimental import pallas as pl
from jax.experimental.pallas import tpu as pltpu
from jax.sharding import PartitionSpec as P

HEAD = 128
GUIDE = 3.0
EPSILON = 1e-06
NEGATIVE = -1e30
BASE = math.log2(math.e) / math.sqrt(HEAD)
BLOCK = 128
PARTS = 8
COLS = 384
SHARE = 4
QUERIES = SHARE * BLOCK
LEAF = BLOCK + 16
BF16 = jnp.bfloat16
F32 = jnp.float32
VMEM = 24 * 1024 * 1024


def nt(a, b):
    return lax.dot_general(a, b, (((1,), (1,)), ((), ())), preferred_element_type=F32)


def nn(a, b):
    return jnp.dot(a, b, preferred_element_type=F32)


def project_kernel(x_ref, mod_ref, w_ref, own_ref, away_ref):
    total = jnp.zeros((BLOCK, 1), F32)
    for b in range(PARTS):
        total += jnp.sum(x_ref[b].astype(F32), axis=-1, keepdims=True)
    average = total * (1.0 / (PARTS * COLS))
    total = jnp.zeros((BLOCK, 1), F32)
    for b in range(PARTS):
        centered = x_ref[b].astype(F32) - average
        total += jnp.sum(centered * centered, axis=-1, keepdims=True)
    inverse = lax.rsqrt(total * (1.0 / (PARTS * COLS)) + EPSILON)
    sums = [jnp.zeros((2 * BLOCK, HEAD), F32) for _ in range(3)]
    for b in range(PARTS):
        cols = slice(b * COLS, (b + 1) * COLS)
        normed = (x_ref[b].astype(F32) - average) * inverse
        both = [
            (normed * (1.0 + mod_ref[1, p : p + 1, cols]) + mod_ref[0, p : p + 1, cols]).astype(BF16)
            for p in range(2)
        ]
        both = jnp.concatenate(both, axis=0)
        for i in range(3):
            sums[i] += nn(both, w_ref[i, cols, :])

    def head_norm(v, scale):
        inverse = lax.rsqrt(jnp.mean(v * v, axis=-1, keepdims=True) + EPSILON) * scale
        return (v * inverse).astype(BF16)

    heads = head_norm(sums[0], BASE), head_norm(sums[1], 1.0), sums[2].astype(BF16)
    guidance = lax.axis_index("guidance")
    for p in range(2):
        rows = slice(p * BLOCK, (p + 1) * BLOCK)

        @pl.when(guidance == p)
        def _():
            for i in range(3):
                own_ref[i] = heads[i][rows]

        @pl.when(guidance != p)
        def _():
            for i in range(3):
                away_ref[i] = heads[i][rows]


def split_level(level):
    high = level.astype(BF16).astype(F32)
    middle = (level - high).astype(BF16).astype(F32)
    return high, middle, level - high - middle


def join(levels, parts):
    top = levels[0]
    for level in levels[1:]:
        top = jnp.maximum(top, level)
    shares = [jnp.exp2(level - top) for level in levels]
    joined = sum(share * part.astype(F32) for share, part in zip(shares, parts))
    return joined / sum(shares)


def attend_kernel(query_ref, fresh_ref, own_ref, far_ref, near_ref, next_ref, mid_ref, text_ref, out_ref):
    own = lax.axis_index("za") * 2 + lax.axis_index("core")
    text_rows = text_ref.shape[1] // SHARE
    first = pl.multiple_of(own * text_rows, text_rows)
    row_block = lax.broadcasted_iota(jnp.int32, (QUERIES, 1), 0) // BLOCK
    other_rows = row_block != own
    lane = lax.broadcasted_iota(jnp.int32, (1, HEAD), 1)
    stats = jnp.zeros((BLOCK, HEAD), F32)
    for h in range(2):
        cols = slice(h * HEAD, (h + 1) * HEAD)
        query = query_ref[:, h].reshape(QUERIES, HEAD)
        scores, values = [], []
        for kv in (own_ref, far_ref):
            scores.append(nt(query, kv[0, :, cols]))
            values.append(kv[1, :, cols])
        scores[0] = jnp.where(other_rows, scores[0], NEGATIVE)
        for kv in (near_ref, next_ref, mid_ref):
            scores.append(nt(query, kv[:, 0, :, cols].reshape(2 * BLOCK, HEAD)))
            values.append(kv[:, 1, :, cols].reshape(2 * BLOCK, HEAD))
        scores.append(jnp.where(other_rows, NEGATIVE, nt(query, fresh_ref[h, 1])))
        values.append(fresh_ref[h, 2])
        scores.append(nt(query, text_ref[0, pl.ds(first, text_rows), cols]))
        values.append(text_ref[1, pl.ds(first, text_rows), cols])
        top = jnp.max(scores[0], axis=-1, keepdims=True)
        for s in scores[1:]:
            top = jnp.maximum(top, jnp.max(s, axis=-1, keepdims=True))
        total = jnp.zeros((QUERIES, 1), F32)
        summed = jnp.zeros((QUERIES, HEAD), F32)
        for s, v in zip(scores, values):
            weights = jnp.exp2(s - top)
            total += jnp.sum(weights, axis=-1, keepdims=True)
            summed += nn(weights.astype(BF16), v)
        summed = (summed / total).astype(BF16)
        pieces = split_level(top + jnp.log2(total))
        for b in range(SHARE):
            rows = slice(b * BLOCK, (b + 1) * BLOCK)
            out_ref[h * SHARE + b, 0:BLOCK, :] = summed[rows]
            for i, piece in enumerate(pieces):
                stats = jnp.where(lane == 16 * (h * SHARE + b) + i, piece[rows], stats)
    stats = jnp.transpose(stats).astype(BF16)
    for d in range(2 * SHARE):
        out_ref[d, BLOCK:LEAF, :] = stats[16 * d : 16 * d + 16]


def output_kernel(reply_ref, mod_ref, w_ref, out_ref):
    stats = [reply_ref[s, BLOCK:LEAF, :].astype(F32) for s in range(2 * SHARE)]
    stats = jnp.transpose(jnp.concatenate(stats, axis=0))
    attended = []
    for p in range(2):
        four = range(p * SHARE, (p + 1) * SHARE)
        levels = [sum(stats[:, 16 * s + i : 16 * s + i + 1] for i in range(3)) for s in four]
        attended.append(join(levels, [reply_ref[s, 0:BLOCK, :] for s in four]).astype(BF16))
    attended = jnp.concatenate(attended, axis=0)
    for b in range(PARTS):
        cols = slice(b * COLS, (b + 1) * COLS)
        branch = nn(attended, w_ref[:, cols])
        mixed = (GUIDE * mod_ref[2, 0:1, cols]) * branch[:BLOCK]
        mixed += ((1.0 - GUIDE) * mod_ref[2, 1:2, cols]) * branch[BLOCK:]
        out_ref[b] = mixed.astype(BF16)


def sum_kernel(parts_ref, out_ref):
    total = jnp.zeros(out_ref.shape, F32)
    for b in range(PARTS):
        total += parts_ref[b].astype(F32)
    out_ref[...] = total.astype(BF16)


def finish_kernel(heads_ref, tokens_ref, out_ref):
    total = tokens_ref[...].astype(F32) + heads_ref[0].astype(F32) + heads_ref[1].astype(F32)
    out_ref[...] = total.astype(BF16)


def call(kernel, shape, *operands):
    out_shape = shape
    if isinstance(shape, tuple):
        out_shape = jax.ShapeDtypeStruct(shape, BF16)
    return pl.pallas_call(
        kernel,
        out_shape=out_shape,
        compiler_params=pltpu.CompilerParams(vmem_limit_bytes=VMEM),
    )(*operands)


def by_core(count):
    return [
        (2 * i + core, 2 * ((i + 1 - 2 * core) % count) + core)
        for i in range(count)
        for core in range(2)
    ]


def together(run, *operands):
    shapes = jax.eval_shape(run, *operands)
    return lax.cond(
        lax.axis_index("za") < 2,
        run,
        lambda *_: jax.tree.map(lambda s: jnp.zeros(s.shape, s.dtype), shapes),
        *operands,
    )


def local(tokens, modulation, w_qkv, w_out, stale, text):
    core = lax.axis_index("core")
    own = stale.reshape(2, BLOCK, 2 * HEAD)
    text = text.reshape(2, -1, 2 * HEAD)
    chip = lax.all_gather(own, "core")
    near = lax.ppermute(chip, ("zf", "core"), by_core(4))
    beside = lax.ppermute(chip, ("zf", "zb", "core"), by_core(8))

    def project(tokens, modulation, w_qkv):
        features = lax.all_to_all(
            jnp.broadcast_to(tokens[None], (PARTS, BLOCK, COLS)), "tensor", 0, 0
        )
        w_qkv = pltpu.with_memory_space_constraint(w_qkv, pltpu.VMEM)
        one_pass = jax.ShapeDtypeStruct((3, BLOCK, HEAD), BF16)
        return call(project_kernel, [one_pass, one_pass], features, modulation, w_qkv)

    own_pass, away = together(project, tokens, modulation, w_qkv)
    away, near, beside = lax.optimization_barrier((away, near, beside))
    mid = lax.ppermute(near, ("zf", "zb", "core"), by_core(8))
    far = lax.ppermute(jnp.where(core == 0, near[0], near[1]), ("zf", "core"), by_core(4))

    def hand_out(own_pass, away):
        heads = lax.all_gather(away, "guidance")
        mine = lax.axis_index("guidance")
        first = jnp.where(mine == 0, own_pass, heads[0])
        second = jnp.where(mine == 0, heads[1], own_pass)
        fresh = jnp.stack([first, second])
        return lax.all_gather(fresh[:, 0], ("za", "core")), fresh

    queries, fresh = together(hand_out, own_pass, away)
    message = call(
        attend_kernel, (2 * SHARE, LEAF, HEAD), queries, fresh, own, far, near, beside, mid, text
    )
    message = lax.all_to_all(message, ("guidance", "za", "core"), 0, 0)
    parts = call(output_kernel, (PARTS, BLOCK, COLS), message, modulation, w_out)
    parts = lax.all_to_all(parts, "tensor", 0, 0)
    heads = lax.all_gather(call(sum_kernel, (BLOCK, COLS), parts), "guidance")
    return call(finish_kernel, (BLOCK, COLS), heads, tokens)


def solution(mesh):
    fine = jax.sharding.Mesh(
        mesh.devices.reshape(4, 2, 2, 2, 8, 2), ("zf", "zb", "za", "core", "tensor", "guidance")
    )
    patch = ("zf", "zb", "za", "core")
    in_specs = (
        P(patch, "tensor"),
        P(),
        P(None, None, ("tensor", "guidance")),
        P(("tensor", "guidance"), None),
        P(None, "guidance", patch, "tensor"),
        P(None, "guidance", None, "tensor"),
    )
    return jax.shard_map(
        local, mesh=fine, in_specs=in_specs, out_specs=P(patch, "tensor"), check_vma=False
    )
```

```python
import math

import jax
import jax.numpy as jnp
from jax import lax
from jax.experimental import pallas as pl
from jax.experimental.pallas import tpu as pltpu
from jax.sharding import PartitionSpec as P

HEAD = 128
GUIDE = 3.0
EPSILON = 1e-06
BASE = math.log2(math.e) / math.sqrt(HEAD)
BLOCK = 128
PARTS = 8
COLS = 384
SHARE = 4
QUERIES = SHARE * BLOCK
LEAF = BLOCK + 16
BF16 = jnp.bfloat16
F32 = jnp.float32
VMEM = 24 * 1024 * 1024


def nt(a, b):
    return lax.dot_general(a, b, (((1,), (1,)), ((), ())), preferred_element_type=F32)


def nn(a, b):
    return jnp.dot(a, b, preferred_element_type=F32)


def project_kernel(x_ref, mod_ref, w_ref, own_ref, away_ref):
    total = jnp.zeros((BLOCK, 1), F32)
    for b in range(PARTS):
        total += jnp.sum(x_ref[b].astype(F32), axis=-1, keepdims=True)
    average = total * (1.0 / (PARTS * COLS))
    total = jnp.zeros((BLOCK, 1), F32)
    for b in range(PARTS):
        centered = x_ref[b].astype(F32) - average
        total += jnp.sum(centered * centered, axis=-1, keepdims=True)
    inverse = lax.rsqrt(total * (1.0 / (PARTS * COLS)) + EPSILON)
    sums = jnp.zeros((2 * BLOCK, 3 * HEAD), F32)
    for b in range(PARTS):
        cols = slice(b * COLS, (b + 1) * COLS)
        normed = (x_ref[b].astype(F32) - average) * inverse
        both = [
            (normed * (1.0 + mod_ref[1, p : p + 1, cols]) + mod_ref[0, p : p + 1, cols]).astype(BF16)
            for p in range(2)
        ]
        both = jnp.concatenate(both, axis=0)
        sums += nn(both, jnp.concatenate([w_ref[i, cols, :] for i in range(3)], axis=1))
    sums = [sums[:, i * HEAD : (i + 1) * HEAD] for i in range(3)]

    def head_norm(v, scale):
        inverse = lax.rsqrt(jnp.mean(v * v, axis=-1, keepdims=True) + EPSILON) * scale
        return (v * inverse).astype(BF16)

    heads = head_norm(sums[0], BASE), head_norm(sums[1], 1.0), sums[2].astype(BF16)
    guidance = lax.axis_index("guidance")
    for p in range(2):
        rows = slice(p * BLOCK, (p + 1) * BLOCK)

        @pl.when(guidance == p)
        def _():
            for i in range(3):
                own_ref[i] = heads[i][rows]

        @pl.when(guidance != p)
        def _():
            for i in range(3):
                away_ref[i] = heads[i][rows]


def split_level(level):
    high = level.astype(BF16).astype(F32)
    middle = (level - high).astype(BF16).astype(F32)
    return high, middle, level - high - middle


def join(levels, parts):
    top = levels[0]
    for level in levels[1:]:
        top = jnp.maximum(top, level)
    shares = [jnp.exp2(level - top) for level in levels]
    joined = sum(share * part.astype(F32) for share, part in zip(shares, parts))
    return joined / sum(shares)


def attend_kernel(query_ref, fresh_ref, own_ref, far_ref, near_ref, next_ref, mid_ref, text_ref, out_ref):
    own = lax.axis_index("za") * 2 + lax.axis_index("core")
    text_rows = text_ref.shape[1] // SHARE
    first = pl.multiple_of(own * text_rows, text_rows)
    row_block = lax.broadcasted_iota(jnp.int32, (QUERIES, 1), 0) // BLOCK
    other_rows = row_block != own
    lane = lax.broadcasted_iota(jnp.int32, (1, HEAD), 1)
    stats = jnp.zeros((BLOCK, HEAD), F32)
    for h in range(2):
        cols = slice(h * HEAD, (h + 1) * HEAD)
        query = query_ref[:, h].reshape(QUERIES, HEAD)
        stale, new = nt(query, own_ref[0, :, cols]), nt(query, fresh_ref[h, 1])
        scores = [jnp.where(other_rows, stale, new), nt(query, far_ref[0, :, cols])]
        values = [None, far_ref[1, :, cols]]
        for kv in (near_ref, next_ref, mid_ref):
            scores.append(nt(query, kv[:, 0, :, cols].reshape(2 * BLOCK, HEAD)))
            values.append(kv[:, 1, :, cols].reshape(2 * BLOCK, HEAD))
        scores.append(nt(query, text_ref[0, pl.ds(first, text_rows), cols]))
        values.append(text_ref[1, pl.ds(first, text_rows), cols])
        top = jnp.max(scores[0], axis=-1, keepdims=True)
        for s in scores[1:]:
            top = jnp.maximum(top, jnp.max(s, axis=-1, keepdims=True))
        total = jnp.zeros((QUERIES, 1), F32)
        summed = jnp.zeros((QUERIES, HEAD), F32)
        for s, v in zip(scores, values):
            weights = jnp.exp2(s - top)
            total += jnp.sum(weights, axis=-1, keepdims=True)
            weights = weights.astype(BF16)
            if v is None:
                nothing = jnp.zeros_like(weights)
                summed += nn(jnp.where(other_rows, weights, nothing), own_ref[1, :, cols])
                summed += nn(jnp.where(other_rows, nothing, weights), fresh_ref[h, 2])
            else:
                summed += nn(weights, v)
        summed = (summed / total).astype(BF16)
        pieces = split_level(top + jnp.log2(total))
        for b in range(SHARE):
            rows = slice(b * BLOCK, (b + 1) * BLOCK)
            out_ref[h * SHARE + b, 0:BLOCK, :] = summed[rows]
            for i, piece in enumerate(pieces):
                stats = jnp.where(lane == 16 * (h * SHARE + b) + i, piece[rows], stats)
    stats = jnp.transpose(stats).astype(BF16)
    for d in range(2 * SHARE):
        out_ref[d, BLOCK:LEAF, :] = stats[16 * d : 16 * d + 16]


def output_kernel(reply_ref, mod_ref, w_ref, out_ref):
    stats = [reply_ref[s, BLOCK:LEAF, :].astype(F32) for s in range(2 * SHARE)]
    stats = jnp.transpose(jnp.concatenate(stats, axis=0))
    attended = []
    for p in range(2):
        four = range(p * SHARE, (p + 1) * SHARE)
        levels = [sum(stats[:, 16 * s + i : 16 * s + i + 1] for i in range(3)) for s in four]
        attended.append(join(levels, [reply_ref[s, 0:BLOCK, :] for s in four]).astype(BF16))
    attended = jnp.concatenate(attended, axis=0)
    for b in range(PARTS):
        cols = slice(b * COLS, (b + 1) * COLS)
        branch = nn(attended, w_ref[:, cols])
        mixed = (GUIDE * mod_ref[2, 0:1, cols]) * branch[:BLOCK]
        mixed += ((1.0 - GUIDE) * mod_ref[2, 1:2, cols]) * branch[BLOCK:]
        out_ref[b] = mixed.astype(BF16)


def sum_kernel(parts_ref, out_ref):
    total = jnp.zeros(out_ref.shape, F32)
    for b in range(PARTS):
        total += parts_ref[b].astype(F32)
    out_ref[...] = total.astype(BF16)


def finish_kernel(heads_ref, tokens_ref, out_ref):
    total = tokens_ref[...].astype(F32) + heads_ref[0].astype(F32) + heads_ref[1].astype(F32)
    out_ref[...] = total.astype(BF16)


def call(kernel, shape, *operands):
    out_shape = shape
    if isinstance(shape, tuple):
        out_shape = jax.ShapeDtypeStruct(shape, BF16)
    return pl.pallas_call(
        kernel,
        out_shape=out_shape,
        compiler_params=pltpu.CompilerParams(vmem_limit_bytes=VMEM),
    )(*operands)


def by_core(count):
    return [
        (2 * i + core, 2 * ((i + 1 - 2 * core) % count) + core)
        for i in range(count)
        for core in range(2)
    ]


def together(run, *operands):
    shapes = jax.eval_shape(run, *operands)
    return lax.cond(
        lax.axis_index("za") < 2,
        run,
        lambda *_: jax.tree.map(lambda s: jnp.zeros(s.shape, s.dtype), shapes),
        *operands,
    )


def local(tokens, modulation, w_qkv, w_out, stale, text):
    core = lax.axis_index("core")
    own = stale.reshape(2, BLOCK, 2 * HEAD)
    text = text.reshape(2, -1, 2 * HEAD)
    chip = lax.all_gather(own, "core")
    near = lax.ppermute(chip, ("zf", "core"), by_core(4))
    beside = lax.ppermute(chip, ("zf", "zb", "core"), by_core(8))

    def project(tokens, modulation, w_qkv):
        features = lax.all_to_all(
            jnp.broadcast_to(tokens[None], (PARTS, BLOCK, COLS)), "tensor", 0, 0
        )
        w_qkv = pltpu.with_memory_space_constraint(w_qkv, pltpu.VMEM)
        one_pass = jax.ShapeDtypeStruct((3, BLOCK, HEAD), BF16)
        return call(project_kernel, [one_pass, one_pass], features, modulation, w_qkv)

    own_pass, away = together(project, tokens, modulation, w_qkv)
    away, near, beside = lax.optimization_barrier((away, near, beside))
    mid = lax.ppermute(near, ("zf", "zb", "core"), by_core(8))
    far = lax.ppermute(jnp.where(core == 0, near[0], near[1]), ("zf", "core"), by_core(4))

    def hand_out(own_pass, away):
        heads = lax.all_gather(away, "guidance")
        mine = lax.axis_index("guidance")
        first = jnp.where(mine == 0, own_pass, heads[0])
        second = jnp.where(mine == 0, heads[1], own_pass)
        fresh = jnp.stack([first, second])
        return lax.all_gather(fresh[:, 0], ("za", "core")), fresh

    queries, fresh = together(hand_out, own_pass, away)
    message = call(
        attend_kernel, (2 * SHARE, LEAF, HEAD), queries, fresh, own, far, near, beside, mid, text
    )
    message = lax.all_to_all(message, ("guidance", "za", "core"), 0, 0)
    parts = call(output_kernel, (PARTS, BLOCK, COLS), message, modulation, w_out)
    parts = lax.all_to_all(parts, "tensor", 0, 0)
    heads = lax.all_gather(call(sum_kernel, (BLOCK, COLS), parts), "guidance")
    return call(finish_kernel, (BLOCK, COLS), heads, tokens)


def solution(mesh):
    fine = jax.sharding.Mesh(
        mesh.devices.reshape(4, 2, 2, 2, 8, 2), ("zf", "zb", "za", "core", "tensor", "guidance")
    )
    patch = ("zf", "zb", "za", "core")
    in_specs = (
        P(patch, "tensor"),
        P(),
        P(None, None, ("tensor", "guidance")),
        P(("tensor", "guidance"), None),
        P(None, "guidance", patch, "tensor"),
        P(None, "guidance", None, "tensor"),
    )
    return jax.shard_map(
        local, mesh=fine, in_specs=in_specs, out_specs=P(patch, "tensor"), check_vma=False
    )
```

```python
import math

import jax
import jax.numpy as jnp
from jax import lax
from jax.experimental import pallas as pl
from jax.experimental.pallas import tpu as pltpu
from jax.sharding import PartitionSpec as P

HEAD = 128
GUIDE = 3.0
EPSILON = 1e-06
BASE = math.log2(math.e) / math.sqrt(HEAD)
BLOCK = 128
PARTS = 8
COLS = 384
SHARE = 4
QUERIES = SHARE * BLOCK
LEAF = BLOCK + 16
BF16 = jnp.bfloat16
F32 = jnp.float32
VMEM = 24 * 1024 * 1024


def nt(a, b):
    return lax.dot_general(a, b, (((1,), (1,)), ((), ())), preferred_element_type=F32)


def nn(a, b):
    return jnp.dot(a, b, preferred_element_type=F32)


def project_kernel(x_ref, mod_ref, w_ref, own_ref, away_ref):
    total = jnp.zeros((BLOCK, 1), F32)
    for b in range(PARTS):
        total += jnp.sum(x_ref[b].astype(F32), axis=-1, keepdims=True)
    average = total * (1.0 / (PARTS * COLS))
    total = jnp.zeros((BLOCK, 1), F32)
    for b in range(PARTS):
        centered = x_ref[b].astype(F32) - average
        total += jnp.sum(centered * centered, axis=-1, keepdims=True)
    inverse = lax.rsqrt(total * (1.0 / (PARTS * COLS)) + EPSILON)
    sums = jnp.zeros((2 * BLOCK, 3 * HEAD), F32)
    for b in range(PARTS):
        cols = slice(b * COLS, (b + 1) * COLS)
        normed = (x_ref[b].astype(F32) - average) * inverse
        both = [
            (normed * (1.0 + mod_ref[1, p : p + 1, cols]) + mod_ref[0, p : p + 1, cols]).astype(BF16)
            for p in range(2)
        ]
        both = jnp.concatenate(both, axis=0)
        sums += nn(both, jnp.concatenate([w_ref[i, cols, :] for i in range(3)], axis=1))
    sums = [sums[:, i * HEAD : (i + 1) * HEAD] for i in range(3)]

    def head_norm(v, scale):
        inverse = lax.rsqrt(jnp.mean(v * v, axis=-1, keepdims=True) + EPSILON) * scale
        return (v * inverse).astype(BF16)

    heads = head_norm(sums[0], BASE), head_norm(sums[1], 1.0), sums[2].astype(BF16)
    guidance = lax.axis_index("guidance")
    for p in range(2):
        rows = slice(p * BLOCK, (p + 1) * BLOCK)

        @pl.when(guidance == p)
        def _():
            for i in range(3):
                own_ref[i] = heads[i][rows]

        @pl.when(guidance != p)
        def _():
            for i in range(3):
                away_ref[i] = heads[i][rows]


def split_level(level):
    high = level.astype(BF16).astype(F32)
    middle = (level - high).astype(BF16).astype(F32)
    return high, middle, level - high - middle


def join(levels, parts):
    top = levels[0]
    for level in levels[1:]:
        top = jnp.maximum(top, level)
    shares = [jnp.exp2(level - top) for level in levels]
    joined = sum(share * part.astype(F32) for share, part in zip(shares, parts))
    return joined / sum(shares)


def attend_kernel(query_ref, fresh_ref, own_ref, far_ref, near_ref, next_ref, mid_ref, text_ref, out_ref):
    own = lax.axis_index("za") * 2 + lax.axis_index("core")
    text_rows = text_ref.shape[1] // SHARE
    first = pl.multiple_of(own * text_rows, text_rows)
    row_block = lax.broadcasted_iota(jnp.int32, (QUERIES, 1), 0) // BLOCK
    other_rows = row_block != own
    lane = lax.broadcasted_iota(jnp.int32, (1, HEAD), 1)
    stats = jnp.zeros((BLOCK, HEAD), F32)
    for h in range(2):
        cols = slice(h * HEAD, (h + 1) * HEAD)
        query = query_ref[:, h].reshape(QUERIES, HEAD)
        stale, new = nt(query, own_ref[0, :, cols]), nt(query, fresh_ref[h, 1])
        scores = [jnp.where(other_rows, stale, new), nt(query, far_ref[0, :, cols])]
        values = [None, far_ref[1, :, cols]]
        for kv in (near_ref, next_ref, mid_ref):
            scores.append(nt(query, kv[:, 0, :, cols].reshape(2 * BLOCK, HEAD)))
            values.append(kv[:, 1, :, cols].reshape(2 * BLOCK, HEAD))
        scores.append(nt(query, text_ref[0, pl.ds(first, text_rows), cols]))
        values.append(text_ref[1, pl.ds(first, text_rows), cols])
        wide = scores[0]
        for s in scores[1:-1]:
            for i in range(0, s.shape[1], HEAD):
                wide = jnp.maximum(wide, s[:, i : i + HEAD])
        top = jnp.max(wide, axis=-1, keepdims=True)
        top = jnp.maximum(top, jnp.max(scores[-1], axis=-1, keepdims=True))
        wide = jnp.zeros((QUERIES, HEAD), F32)
        total = jnp.zeros((QUERIES, 1), F32)
        summed = jnp.zeros((QUERIES, HEAD), F32)
        for s, v in zip(scores, values):
            weights = jnp.exp2(s - top)
            if s.shape[1] % HEAD:
                total += jnp.sum(weights, axis=-1, keepdims=True)
            else:
                for i in range(0, s.shape[1], HEAD):
                    wide += weights[:, i : i + HEAD]
            weights = weights.astype(BF16)
            if v is None:
                nothing = jnp.zeros_like(weights)
                summed += nn(jnp.where(other_rows, weights, nothing), own_ref[1, :, cols])
                summed += nn(jnp.where(other_rows, nothing, weights), fresh_ref[h, 2])
            else:
                summed += nn(weights, v)
        total += jnp.sum(wide, axis=-1, keepdims=True)
        summed = (summed / total).astype(BF16)
        pieces = split_level(top + jnp.log2(total))
        for b in range(SHARE):
            rows = slice(b * BLOCK, (b + 1) * BLOCK)
            out_ref[h * SHARE + b, 0:BLOCK, :] = summed[rows]
            for i, piece in enumerate(pieces):
                stats = jnp.where(lane == 16 * (h * SHARE + b) + i, piece[rows], stats)
    stats = jnp.transpose(stats).astype(BF16)
    for d in range(2 * SHARE):
        out_ref[d, BLOCK:LEAF, :] = stats[16 * d : 16 * d + 16]


def output_kernel(reply_ref, mod_ref, w_ref, out_ref):
    stats = [reply_ref[s, BLOCK:LEAF, :].astype(F32) for s in range(2 * SHARE)]
    stats = jnp.transpose(jnp.concatenate(stats, axis=0))
    attended = []
    for p in range(2):
        four = range(p * SHARE, (p + 1) * SHARE)
        levels = [sum(stats[:, 16 * s + i : 16 * s + i + 1] for i in range(3)) for s in four]
        attended.append(join(levels, [reply_ref[s, 0:BLOCK, :] for s in four]).astype(BF16))
    attended = jnp.concatenate(attended, axis=0)
    for b in range(PARTS):
        cols = slice(b * COLS, (b + 1) * COLS)
        branch = nn(attended, w_ref[:, cols])
        mixed = (GUIDE * mod_ref[2, 0:1, cols]) * branch[:BLOCK]
        mixed += ((1.0 - GUIDE) * mod_ref[2, 1:2, cols]) * branch[BLOCK:]
        out_ref[b] = mixed.astype(BF16)


def sum_kernel(parts_ref, out_ref):
    total = jnp.zeros(out_ref.shape, F32)
    for b in range(PARTS):
        total += parts_ref[b].astype(F32)
    out_ref[...] = total.astype(BF16)


def finish_kernel(heads_ref, tokens_ref, out_ref):
    total = tokens_ref[...].astype(F32) + heads_ref[0].astype(F32) + heads_ref[1].astype(F32)
    out_ref[...] = total.astype(BF16)


def call(kernel, shape, *operands):
    out_shape = shape
    if isinstance(shape, tuple):
        out_shape = jax.ShapeDtypeStruct(shape, BF16)
    return pl.pallas_call(
        kernel,
        out_shape=out_shape,
        compiler_params=pltpu.CompilerParams(vmem_limit_bytes=VMEM),
    )(*operands)


def by_core(count):
    return [
        (2 * i + core, 2 * ((i + 1 - 2 * core) % count) + core)
        for i in range(count)
        for core in range(2)
    ]


def together(run, *operands):
    shapes = jax.eval_shape(run, *operands)
    return lax.cond(
        lax.axis_index("za") < 2,
        run,
        lambda *_: jax.tree.map(lambda s: jnp.zeros(s.shape, s.dtype), shapes),
        *operands,
    )


def local(tokens, modulation, w_qkv, w_out, stale, text):
    core = lax.axis_index("core")
    own = stale.reshape(2, BLOCK, 2 * HEAD)
    text = text.reshape(2, -1, 2 * HEAD)
    chip = lax.all_gather(own, "core")
    near = lax.ppermute(chip, ("zf", "core"), by_core(4))
    beside = lax.ppermute(chip, ("zf", "zb", "core"), by_core(8))

    def project(tokens, modulation, w_qkv):
        features = lax.all_to_all(
            jnp.broadcast_to(tokens[None], (PARTS, BLOCK, COLS)), "tensor", 0, 0
        )
        w_qkv = pltpu.with_memory_space_constraint(w_qkv, pltpu.VMEM)
        one_pass = jax.ShapeDtypeStruct((3, BLOCK, HEAD), BF16)
        return call(project_kernel, [one_pass, one_pass], features, modulation, w_qkv)

    own_pass, away = together(project, tokens, modulation, w_qkv)
    away, near, beside = lax.optimization_barrier((away, near, beside))
    mid = lax.ppermute(near, ("zf", "zb", "core"), by_core(8))
    far = lax.ppermute(lax.dynamic_index_in_dim(near, core, 0, keepdims=False), ("zf", "core"), by_core(4))

    def hand_out(own_pass, away):
        heads = lax.all_gather(away, "guidance")
        mine = lax.axis_index("guidance")
        first = jnp.where(mine == 0, own_pass, heads[0])
        second = jnp.where(mine == 0, heads[1], own_pass)
        fresh = jnp.stack([first, second])
        return lax.all_gather(fresh[:, 0], ("za", "core")), fresh

    queries, fresh = together(hand_out, own_pass, away)
    message = call(
        attend_kernel, (2 * SHARE, LEAF, HEAD), queries, fresh, own, far, near, beside, mid, text
    )
    message = lax.all_to_all(message, ("guidance", "za", "core"), 0, 0)
    parts = call(output_kernel, (PARTS, BLOCK, COLS), message, modulation, w_out)
    parts = lax.all_to_all(parts, "tensor", 0, 0)
    heads = lax.all_gather(call(sum_kernel, (BLOCK, COLS), parts), "guidance")
    return call(finish_kernel, (BLOCK, COLS), heads, tokens)


def solution(mesh):
    fine = jax.sharding.Mesh(
        mesh.devices.reshape(4, 2, 2, 2, 8, 2), ("zf", "zb", "za", "core", "tensor", "guidance")
    )
    patch = ("zf", "zb", "za", "core")
    in_specs = (
        P(patch, "tensor"),
        P(),
        P(None, None, ("tensor", "guidance")),
        P(("tensor", "guidance"), None),
        P(None, "guidance", patch, "tensor"),
        P(None, "guidance", None, "tensor"),
    )
    return jax.shard_map(
        local, mesh=fine, in_specs=in_specs, out_specs=P(patch, "tensor"), check_vma=False
    )
```

```python
import math

import jax
import jax.numpy as jnp
from jax import lax
from jax.experimental import pallas as pl
from jax.experimental.pallas import tpu as pltpu
from jax.sharding import PartitionSpec as P

HEAD = 128
GUIDE = 3.0
EPSILON = 1e-06
BASE = math.log2(math.e) / math.sqrt(HEAD)
BLOCK = 128
PARTS = 8
COLS = 384
SHARE = 4
QUERIES = SHARE * BLOCK
LEAF = BLOCK + 16
BF16 = jnp.bfloat16
F32 = jnp.float32
VMEM = 24 * 1024 * 1024


def nt(a, b):
    return lax.dot_general(a, b, (((1,), (1,)), ((), ())), preferred_element_type=F32)


def nn(a, b):
    return jnp.dot(a, b, preferred_element_type=F32)


def project_kernel(x_ref, mod_ref, w_ref, own_ref, away_ref):
    total = jnp.zeros((BLOCK, 1), F32)
    for b in range(PARTS):
        total += jnp.sum(x_ref[b].astype(F32), axis=-1, keepdims=True)
    average = total * (1.0 / (PARTS * COLS))
    total = jnp.zeros((BLOCK, 1), F32)
    for b in range(PARTS):
        centered = x_ref[b].astype(F32) - average
        total += jnp.sum(centered * centered, axis=-1, keepdims=True)
    inverse = lax.rsqrt(total * (1.0 / (PARTS * COLS)) + EPSILON)
    sums = jnp.zeros((2 * BLOCK, 3 * HEAD), F32)
    for b in range(PARTS):
        cols = slice(b * COLS, (b + 1) * COLS)
        normed = (x_ref[b].astype(F32) - average) * inverse
        both = [
            (normed * (1.0 + mod_ref[1, p : p + 1, cols]) + mod_ref[0, p : p + 1, cols]).astype(BF16)
            for p in range(2)
        ]
        both = jnp.concatenate(both, axis=0)
        sums += nn(both, jnp.concatenate([w_ref[i, cols, :] for i in range(3)], axis=1))
    sums = [sums[:, i * HEAD : (i + 1) * HEAD] for i in range(3)]

    def head_norm(v, scale):
        inverse = lax.rsqrt(jnp.mean(v * v, axis=-1, keepdims=True) + EPSILON) * scale
        return (v * inverse).astype(BF16)

    heads = head_norm(sums[0], BASE), head_norm(sums[1], 1.0), sums[2].astype(BF16)
    guidance = lax.axis_index("guidance")
    for p in range(2):
        rows = slice(p * BLOCK, (p + 1) * BLOCK)

        @pl.when(guidance == p)
        def _():
            for i in range(3):
                own_ref[i] = heads[i][rows]

        @pl.when(guidance != p)
        def _():
            for i in range(3):
                away_ref[i] = heads[i][rows]


def split_level(level):
    high = level.astype(BF16).astype(F32)
    middle = (level - high).astype(BF16).astype(F32)
    return high, middle, level - high - middle


def join(levels, parts):
    top = levels[0]
    for level in levels[1:]:
        top = jnp.maximum(top, level)
    shares = [jnp.exp2(level - top) for level in levels]
    joined = sum(share * part.astype(F32) for share, part in zip(shares, parts))
    return joined * (1.0 / sum(shares))


def attend_kernel(query_ref, fresh_ref, own_ref, far_ref, near_ref, next_ref, mid_ref, text_ref, out_ref):
    own = lax.axis_index("za") * 2 + lax.axis_index("core")
    text_rows = text_ref.shape[1] // SHARE
    first = pl.multiple_of(own * text_rows, text_rows)
    row_block = lax.broadcasted_iota(jnp.int32, (QUERIES, 1), 0) // BLOCK
    other_rows = row_block != own
    lane = lax.broadcasted_iota(jnp.int32, (1, HEAD), 1)
    stats = jnp.zeros((BLOCK, HEAD), F32)
    for h in range(2):
        cols = slice(h * HEAD, (h + 1) * HEAD)
        query = query_ref[:, h].reshape(QUERIES, HEAD)
        stale, new = nt(query, own_ref[0, :, cols]), nt(query, fresh_ref[h, 1])
        scores = [jnp.where(other_rows, stale, new), nt(query, far_ref[0, :, cols])]
        values = [None, far_ref[1, :, cols]]
        for kv in (near_ref, next_ref, mid_ref):
            scores.append(nt(query, kv[:, 0, :, cols].reshape(2 * BLOCK, HEAD)))
            values.append(kv[:, 1, :, cols].reshape(2 * BLOCK, HEAD))
        scores.append(nt(query, text_ref[0, pl.ds(first, text_rows), cols]))
        values.append(text_ref[1, pl.ds(first, text_rows), cols])
        wide = scores[0]
        for s in scores[1:-1]:
            for i in range(0, s.shape[1], HEAD):
                wide = jnp.maximum(wide, s[:, i : i + HEAD])
        top = jnp.max(wide, axis=-1, keepdims=True)
        top = jnp.maximum(top, jnp.max(scores[-1], axis=-1, keepdims=True))
        wide = jnp.zeros((QUERIES, HEAD), F32)
        total = jnp.zeros((QUERIES, 1), F32)
        summed = jnp.zeros((QUERIES, HEAD), F32)
        for s, v in zip(scores, values):
            weights = jnp.exp2(s - top)
            if s.shape[1] % HEAD:
                total += jnp.sum(weights, axis=-1, keepdims=True)
            else:
                for i in range(0, s.shape[1], HEAD):
                    wide += weights[:, i : i + HEAD]
            weights = weights.astype(BF16)
            if v is None:
                nothing = jnp.zeros_like(weights)
                summed += nn(jnp.where(other_rows, weights, nothing), own_ref[1, :, cols])
                summed += nn(jnp.where(other_rows, nothing, weights), fresh_ref[h, 2])
            else:
                summed += nn(weights, v)
        total += jnp.sum(wide, axis=-1, keepdims=True)
        summed = (summed * (1.0 / total)).astype(BF16)
        pieces = split_level(top + jnp.log2(total))
        for b in range(SHARE):
            rows = slice(b * BLOCK, (b + 1) * BLOCK)
            out_ref[h * SHARE + b, 0:BLOCK, :] = summed[rows]
            for i, piece in enumerate(pieces):
                stats = jnp.where(lane == 16 * (h * SHARE + b) + i, piece[rows], stats)
    stats = jnp.transpose(stats).astype(BF16)
    for d in range(2 * SHARE):
        out_ref[d, BLOCK:LEAF, :] = stats[16 * d : 16 * d + 16]


def output_kernel(reply_ref, mod_ref, w_ref, out_ref):
    stats = [reply_ref[s, BLOCK:LEAF, :].astype(F32) for s in range(2 * SHARE)]
    stats = jnp.transpose(jnp.concatenate(stats, axis=0))
    attended = []
    for p in range(2):
        four = range(p * SHARE, (p + 1) * SHARE)
        levels = [sum(stats[:, 16 * s + i : 16 * s + i + 1] for i in range(3)) for s in four]
        attended.append(join(levels, [reply_ref[s, 0:BLOCK, :] for s in four]).astype(BF16))
    attended = jnp.concatenate(attended, axis=0)
    for b in range(PARTS):
        cols = slice(b * COLS, (b + 1) * COLS)
        branch = nn(attended, w_ref[:, cols])
        mixed = (GUIDE * mod_ref[2, 0:1, cols]) * branch[:BLOCK]
        mixed += ((1.0 - GUIDE) * mod_ref[2, 1:2, cols]) * branch[BLOCK:]
        out_ref[b] = mixed.astype(BF16)


def sum_kernel(parts_ref, out_ref):
    total = jnp.zeros(out_ref.shape, F32)
    for b in range(PARTS):
        total += parts_ref[b].astype(F32)
    out_ref[...] = total.astype(BF16)


def finish_kernel(heads_ref, tokens_ref, out_ref):
    total = tokens_ref[...].astype(F32) + heads_ref[0].astype(F32) + heads_ref[1].astype(F32)
    out_ref[...] = total.astype(BF16)


def call(kernel, shape, *operands):
    out_shape = shape
    if isinstance(shape, tuple):
        out_shape = jax.ShapeDtypeStruct(shape, BF16)
    return pl.pallas_call(
        kernel,
        out_shape=out_shape,
        compiler_params=pltpu.CompilerParams(vmem_limit_bytes=VMEM),
    )(*operands)


def by_core(count):
    return [
        (2 * i + core, 2 * ((i + 1 - 2 * core) % count) + core)
        for i in range(count)
        for core in range(2)
    ]


def together(run, *operands):
    shapes = jax.eval_shape(run, *operands)
    return lax.cond(
        lax.axis_index("za") < 2,
        run,
        lambda *_: jax.tree.map(lambda s: jnp.zeros(s.shape, s.dtype), shapes),
        *operands,
    )


def local(tokens, modulation, w_qkv, w_out, stale, text):
    core = lax.axis_index("core")
    own = stale.reshape(2, BLOCK, 2 * HEAD)
    text = text.reshape(2, -1, 2 * HEAD)
    chip = lax.all_gather(own, "core")
    near = lax.ppermute(chip, ("zf", "core"), by_core(4))
    beside = lax.ppermute(chip, ("zf", "zb", "core"), by_core(8))

    def project(tokens, modulation, w_qkv):
        features = lax.all_to_all(
            jnp.broadcast_to(tokens[None], (PARTS, BLOCK, COLS)), "tensor", 0, 0
        )
        w_qkv = pltpu.with_memory_space_constraint(w_qkv, pltpu.VMEM)
        one_pass = jax.ShapeDtypeStruct((3, BLOCK, HEAD), BF16)
        return call(project_kernel, [one_pass, one_pass], features, modulation, w_qkv)

    own_pass, away = together(project, tokens, modulation, w_qkv)
    away, near, beside = lax.optimization_barrier((away, near, beside))
    mid = lax.ppermute(near, ("zf", "zb", "core"), by_core(8))
    far = lax.ppermute(lax.dynamic_index_in_dim(near, core, 0, keepdims=False), ("zf", "core"), by_core(4))

    def hand_out(own_pass, away):
        heads = lax.all_gather(away, "guidance")
        mine = lax.axis_index("guidance")
        first = jnp.where(mine == 0, own_pass, heads[0])
        second = jnp.where(mine == 0, heads[1], own_pass)
        fresh = jnp.stack([first, second])
        return lax.all_gather(fresh[:, 0], ("za", "core")), fresh

    queries, fresh = together(hand_out, own_pass, away)
    message = call(
        attend_kernel, (2 * SHARE, LEAF, HEAD), queries, fresh, own, far, near, beside, mid, text
    )
    message = lax.all_to_all(message, ("guidance", "za", "core"), 0, 0)
    parts = call(output_kernel, (PARTS, BLOCK, COLS), message, modulation, w_out)
    parts = lax.all_to_all(parts, "tensor", 0, 0)
    heads = lax.all_gather(call(sum_kernel, (BLOCK, COLS), parts), "guidance")
    return call(finish_kernel, (BLOCK, COLS), heads, tokens)


def solution(mesh):
    fine = jax.sharding.Mesh(
        mesh.devices.reshape(4, 2, 2, 2, 8, 2), ("zf", "zb", "za", "core", "tensor", "guidance")
    )
    patch = ("zf", "zb", "za", "core")
    in_specs = (
        P(patch, "tensor"),
        P(),
        P(None, None, ("tensor", "guidance")),
        P(("tensor", "guidance"), None),
        P(None, "guidance", patch, "tensor"),
        P(None, "guidance", None, "tensor"),
    )
    return jax.shard_map(
        local, mesh=fine, in_specs=in_specs, out_specs=P(patch, "tensor"), check_vma=False
    )
```
